256 devices in a mesh: seq: 8 (over z), nbr: 32 (over y, x, core).
Axes of the slice: x: 4, y: 4, z: 8, core: 2. Of those that a mesh axis runs over, the one named last changes fastest.
Arguments:
- queries: bfloat16 [32768, 2048], P(('seq', 'nbr')), may hold values from -360 to 360
- d_context: bfloat16 [32768, 2048], P(('seq', 'nbr')), may hold values from -6 to 6
- database: bfloat16 [1024, 128, 1024], P(('seq', 'nbr')), may hold values from -6 to 6
- neighbour_source: int32 [512, 2], P(('seq', 'nbr')), may hold values from 0 to 7, all different within a row; in each aligned block of 2 rows (0 to 1, 2 to 3, ...) at most 2 rows name the same one
- neighbour_slot: int32 [512, 2], P(('seq', 'nbr')), may hold values from 0 to 3
- enc_gain: float32 [1024], replicated, may hold values from 0.1 to 1.9
- kv_weight: bfloat16 [1024, 4096], P('nbr'), may hold values from -0.1875 to 0.1875
Outputs:
- context: bfloat16 [32768, 2048], P(('seq', 'nbr'))
- d_queries: bfloat16 [32768, 2048], P(('seq', 'nbr'))
- d_kv_weight: float32 [1024, 4096], P('nbr')
- d_database: float32 [1024, 128, 1024], P(('seq', 'nbr'))
The draws below stay inside these ranges and needn't reach their ends.
Inputs may be any that keep to these rules, and one draw needn't show every extreme that they name: `neighbour_source`: A span's 2 neighbours lie on different devices; among the neighbours of one device's spans at most 2 lie on any one device, and exactly 2 on one device in some or all devices.
All inputs are finite; a program needn't handle non-finite values.
Results may differ from the reference program's by a relative error of at most 0.024.
The reference program's roundings to bfloat16 on the way (of `fetched`, `normed`, `projected`, `probs_half`, `d_scores`, `d_projected` and `d_fetched`) count: a program that leaves them out, or rounds other values in their place, can miss the bound.
Values may be sent and summed in bfloat16 or wider, within the bound.
No kernel may reach another device: no remote copies, remote signals or barrier semaphores. Data moves between devices by JAX's collectives and lax.ppermute only.
A program may use at most 128 MiB of HBM per device.

```python
import math
import jax
import jax.numpy as jnp
import numpy as np
from jax import lax

D_ENC = 1024
HEADS = 16
HEAD_DIM = 128
SPAN = 64
NBR_LEN = 128
K_NBR = 2
CH_DEV = 2
DB_DEV = 4
CAP = 2
KV_WIDTH = 2048
SPANS = 512
TOKENS = 32768
DB_ROWS = 1024
N_SEQ = 8
N_NBR = 32
DEVICES = 256


def draw_queries(key, part):
    key = jax.random.fold_in(key, 7)
    normal_key = jax.random.fold_in(key, 0)
    normal_part = jnp.clip(jax.random.normal(normal_key, (TOKENS, KV_WIDTH), jnp.float32), -6.0, 6.0)
    return normal_part.astype(jnp.bfloat16)


def plant(array, key, least, top_value):
    spot = [jax.random.randint(jax.random.fold_in(key, axis), (), 0, length) for axis, length in enumerate(array.shape)]
    main_axis = array.shape.index(max(array.shape))
    beside = spot[:main_axis] + [(spot[main_axis] + 1) % array.shape[main_axis]] + spot[main_axis + 1:]
    return array.at[tuple(spot)].set(least).at[tuple(beside)].set(top_value)


def steps_of(own_key, shape, shards, least, top_value):
    def one(axis_at, parts):
        heights = jax.random.uniform(jax.random.fold_in(jax.random.fold_in(own_key, 6), axis_at), (parts,), jnp.float32, least / len(shards), top_value / len(shards))
        return jnp.repeat(jnp.exp(heights), shape[axis_at] // parts).reshape((-1,) + (1,) * (len(shape) - axis_at - 1))

    level = one(*shards[0])
    for cut in shards[1:]:
        level = level * one(*cut)
    return level


def assign_block(rng, own, number, rows, count, top, most, lean):
    order = jax.random.permutation(rng, count)
    crowded, ordinary = shares(count, rows * top, most, lean, True), shares(count, rows * top, most, lean, False)
    places = jnp.arange(count)

    def named(sizes, rotation):
        used = int((sizes > 0).sum())
        fixed = max(1, used // 4)
        passed = fixed + (places - fixed + rotation * (used - fixed)) % max(1, count - fixed)
        return jnp.zeros((count,), jnp.int32).at[order[jnp.where(places < fixed, places, passed)]].set(jnp.asarray(sizes, jnp.int32))

    sizes = jnp.where(number % 4 == 0, named(crowded, number // 4), named(ordinary, number - number // 4 - 1))
    mixed = jax.random.permutation(jax.random.fold_in(own, 3), count)
    giver, receiver = mixed[0:count // 2 * 2:2], mixed[1:count // 2 * 2:2]
    slack = jnp.minimum(sizes[giver] - 1, most - sizes[receiver]) // 2
    slack = jnp.where((giver == order[0]) | (receiver == order[0]) | (sizes[receiver] == 0), 0, jnp.maximum(slack, 0))
    passed = jax.random.randint(jax.random.fold_in(own, 4), (count // 2,), 0, 1 << 20) % (slack + 1)
    sizes = sizes.at[giver].add(-passed).at[receiver].add(passed)
    labels = jnp.searchsorted(jnp.cumsum(sizes), jnp.arange(rows * top), side="right").astype(jnp.int32)
    grid = labels.reshape(top, rows).T
    grid = grid[jax.random.permutation(jax.random.fold_in(own, 1), rows)]
    rotation = jax.random.randint(jax.random.fold_in(own, 2), (rows, 1), 0, top)
    return jnp.take_along_axis(grid, (jnp.arange(top)[None, :] + rotation) % top, axis=1)


def shares(number_of, total, bound, slope, full):
    loads = [(1 << 20) // math.isqrt(rank ** slope) + 1 for rank in range(1, number_of + 1)]
    largest = bound if full else min(bound, max(-(-total // number_of), total * loads[0] // sum(loads)))
    least = 1 if total - largest >= number_of - 1 else 0
    counts, surplus = [largest] + [least] * (number_of - 1), total - largest - least * (number_of - 1)
    while surplus > 0:
        movable = [i for i in range(1, number_of) if counts[i] < largest] or [i for i in range(1, number_of) if counts[i] < bound]
        pool, left = sum([loads[i] for i in movable]), surplus
        for i in movable:
            addition = min(bound - counts[i], max(1, left * loads[i] // pool), surplus)
            counts[i] = counts[i] + addition
            surplus = surplus - addition
    return np.array(counts)


def gaussian(key, dims, scale, most, shards=(), held_as=jnp.bfloat16):
    result = scale * jax.random.normal(key, dims, jnp.float32)
    if shards:
        result = result * steps_of(key, dims, shards, -0.22, 0.18)
    return jnp.clip(result, -most, most).astype(held_as)


def setup_inputs(seed: int = 0) -> dict:
    streams_of = jax.random.split(jax.random.key(seed), 8)
    queries = draw_queries(jax.random.fold_in(streams_of[7], 71), 0)
    d_context = gaussian(streams_of[1], (TOKENS, KV_WIDTH), 1.0, 6.0, ((0, 256),))
    database = gaussian(streams_of[2], (DB_ROWS, NBR_LEN, D_ENC), 1.0, 6.0, ((0, 256),))
    neighbour_source_keys = jax.random.split(jax.random.fold_in(streams_of[3], 1), SPANS // CH_DEV)
    neighbour_source_turns = jax.random.permutation(jax.random.fold_in(streams_of[3], 3), SPANS // CH_DEV)
    neighbour_source = jax.vmap(lambda own, number: assign_block(jax.random.fold_in(streams_of[3], 2), own, number, CH_DEV, N_SEQ, K_NBR, CAP, 2))(neighbour_source_keys, neighbour_source_turns).reshape((SPANS, K_NBR))
    neighbour_slot = plant(jax.random.randint(streams_of[4], (SPANS, K_NBR), 0, DB_DEV), jax.random.fold_in(streams_of[4], 1), 0, DB_DEV - 1).astype(jnp.int32)
    enc_gain = jnp.clip(1.0 + 0.18 * jax.random.normal(streams_of[5], (D_ENC,), jnp.float32), 0.1, 1.9)
    kv_weight = gaussian(streams_of[6], (D_ENC, 2 * KV_WIDTH), D_ENC ** -0.5, 0.1875, ((0, 32),))
    return dict(queries=queries, d_context=d_context, database=database, neighbour_source=neighbour_source, neighbour_slot=neighbour_slot, enc_gain=enc_gain, kv_weight=kv_weight)


EPSILON = 1e-06

def norm_rows(field_rows, enc_gain):
    mean_square = lax.optimization_barrier(jnp.mean(field_rows * field_rows, axis=-1, keepdims=True))
    return field_rows * lax.rsqrt(mean_square + EPSILON) * enc_gain

def reference(queries, d_context, database, neighbour_source, neighbour_slot, enc_gain, kv_weight):
    request_count = K_NBR * CH_DEV
    scale_factor = HEAD_DIM ** (-0.5)
    query_blocks = queries.reshape(DEVICES, CH_DEV, SPAN, HEADS, HEAD_DIM)
    grad_blocks = d_context.reshape(DEVICES, CH_DEV, SPAN, HEADS, HEAD_DIM)
    source_blocks = neighbour_source.reshape(DEVICES, request_count)
    slot_blocks = neighbour_slot.reshape(DEVICES, request_count)
    device_ids = jnp.arange(DEVICES, dtype=jnp.int32)

    def per_device(carry, inputs):
        weight_sum, database_sum = carry
        query_span, grad_span, source_ids, slot_ids, device_id = inputs
        row_ids = ((source_ids * N_NBR + device_id % N_NBR) * DB_DEV + slot_ids).astype(jnp.int32)
        fetched = database[row_ids].astype(jnp.float32)
        normed = norm_rows(fetched, enc_gain).astype(jnp.bfloat16)
        flat_normed = normed.reshape(request_count * NBR_LEN, D_ENC)
        projected = jnp.dot(flat_normed, kv_weight, preferred_element_type=jnp.float32).astype(jnp.bfloat16)
        key_rows = projected[:, :KV_WIDTH].reshape(CH_DEV, K_NBR * NBR_LEN, HEADS, HEAD_DIM).astype(jnp.float32)
        value_rows = projected[:, KV_WIDTH:].reshape(CH_DEV, K_NBR * NBR_LEN, HEADS, HEAD_DIM).astype(jnp.float32)
        query_wide = query_span.astype(jnp.float32)
        grad_wide = grad_span.astype(jnp.float32)
        scores = jnp.einsum('cqhd,ckhd->chqk', query_wide, key_rows) * scale_factor
        highest = lax.optimization_barrier(jnp.max(scores, axis=-1, keepdims=True))
        expanded = jnp.exp(scores - highest)
        probs = expanded / lax.optimization_barrier(jnp.sum(expanded, axis=-1, keepdims=True))
        probs_half = probs.astype(jnp.bfloat16)
        context_span = jnp.einsum('chqk,ckhd->cqhd', probs_half.astype(jnp.float32), value_rows).astype(jnp.bfloat16)
        d_probs = jnp.einsum('cqhd,ckhd->chqk', grad_wide, value_rows)
        delta = lax.optimization_barrier(jnp.sum(probs * d_probs, axis=-1, keepdims=True))
        d_scores = (probs * (d_probs - delta) * scale_factor).astype(jnp.bfloat16)
        d_scores_wide = d_scores.astype(jnp.float32)
        d_query_span = jnp.einsum('chqk,ckhd->cqhd', d_scores_wide, key_rows).astype(jnp.bfloat16)
        d_keys = jnp.einsum('chqk,cqhd->ckhd', d_scores_wide, query_wide).astype(jnp.bfloat16)
        d_values = jnp.einsum('chqk,cqhd->ckhd', probs_half.astype(jnp.float32), grad_wide).astype(jnp.bfloat16)
        d_projected = jnp.concatenate([d_keys.reshape(request_count * NBR_LEN, KV_WIDTH), d_values.reshape(request_count * NBR_LEN, KV_WIDTH)], axis=1)
        weight_term = lax.dot_general(flat_normed, d_projected, (((0,), (0,)), ((), ())), preferred_element_type=jnp.float32)
        weight_term = lax.optimization_barrier(weight_term.astype(jnp.bfloat16)).astype(jnp.float32)
        d_normed = lax.dot_general(d_projected, kv_weight, (((1,), (1,)), ((), ())), preferred_element_type=jnp.float32)
        unused, pullback = jax.vjp(lambda field_rows: norm_rows(field_rows, enc_gain), fetched)
        d_fetched = pullback(d_normed.reshape(request_count, NBR_LEN, D_ENC))[0].astype(jnp.bfloat16)
        d_fetched = lax.optimization_barrier(d_fetched).astype(jnp.float32)
        database_sum = database_sum.at[row_ids].add(d_fetched)
        return ((weight_sum + weight_term, database_sum), (context_span, d_query_span))
    start_carry = (jnp.zeros((D_ENC, 2 * KV_WIDTH), jnp.float32), jnp.zeros((DB_ROWS, NBR_LEN, D_ENC), jnp.float32))
    (d_kv_weight, d_database), (context, d_queries) = lax.scan(per_device, start_carry, (query_blocks, grad_blocks, source_blocks, slot_blocks, device_ids))
    context = context.reshape(TOKENS, KV_WIDTH)
    d_queries = d_queries.reshape(TOKENS, KV_WIDTH)
    return (context, d_queries, d_kv_weight, d_database)
```

```python
import functools

import jax
import jax.numpy as jnp
from jax import lax
from jax.experimental import pallas as pl
from jax.experimental.pallas import tpu as pltpu
from jax.sharding import PartitionSpec as P

HEAD_DIM = 128
K_NBR = 2
EPSILON = 1e-06
HEADS_STEP = 2
X_CHIPS = 4
Y_CHIPS = 4
F32 = jnp.float32
BF16 = jnp.bfloat16


def mm(a, b, ca, cb):
    return lax.dot_general(a, b, (((ca,), (cb,)), ((), ())), preferred_element_type=F32)


def pick_kernel(ids_ref, stored_ref, out_ref, *, peers, stored, requests, piece):
    for peer in range(peers):
        for r in range(requests):
            row = ids_ref[peer * requests + r]
            source = lax.div(row, stored)
            start = pl.multiple_of(lax.rem(row, stored) * piece, piece)
            out_ref[peer, pl.ds(r * piece, piece), :] = stored_ref[source, pl.ds(start, piece), :]


def sum_kernel(ids_ref, grads_ref, out_ref, total_ref, *, peers, requests, piece):
    total_ref[...] = jnp.zeros_like(total_ref)
    for peer in range(peers):
        for r in range(requests):
            row = ids_ref[peer * requests + r]
            total_ref[row] += grads_ref[peer, pl.ds(r * piece, piece), :].astype(F32)
    out_ref[...] = total_ref[...].astype(BF16).reshape(out_ref.shape)


def main_kernel(
    core_ref,
    rows_ref,
    gain_ref,
    wk_ref,
    wv_ref,
    q_ref,
    g_ref,
    ctx_ref,
    dq_ref,
    own_k_ref,
    oth_k_ref,
    own_v_ref,
    oth_v_ref,
    dfet_ref,
    normed_ref,
    normed_t_ref,
    dnormed_ref,
    dk_ref,
    dv_ref,
    *,
    spans,
    span_length,
):
    step = pl.program_id(0)
    scale_factor = HEAD_DIM ** (-0.5)
    positions = normed_ref.shape[0] // spans
    width = rows_ref.shape[-1]
    gain = gain_ref[...]

    def wide_rows(c):
        return rows_ref[:, c].astype(F32).reshape(positions, width)

    @pl.when(step == 0)
    def _():
        for c in range(spans):
            x = wide_rows(c)
            r = lax.rsqrt(jnp.mean(x * x, axis=-1, keepdims=True) + EPSILON)
            normed = (x * r * gain).astype(BF16)
            normed_ref[pl.ds(c * positions, positions), :] = normed
            normed_t_ref[:, pl.ds(c * positions, positions)] = normed.T
        dnormed_ref[...] = jnp.zeros_like(dnormed_ref)

    normed = normed_ref[...]
    keys = mm(normed, wk_ref[...], 1, 0).astype(BF16)
    values = mm(normed, wv_ref[...], 1, 0).astype(BF16)
    for c in range(spans):
        for h in range(HEADS_STEP):
            toks = slice(c * span_length, (c + 1) * span_length)
            poss = slice(c * positions, (c + 1) * positions)
            cols = slice(h * HEAD_DIM, (h + 1) * HEAD_DIM)
            q = q_ref[toks, cols]
            g = g_ref[toks, cols]
            k = keys[poss, cols]
            v = values[poss, cols]
            scores = mm(q, k, 1, 1) * scale_factor
            expanded = jnp.exp(scores - jnp.max(scores, axis=-1, keepdims=True))
            probs = expanded / jnp.sum(expanded, axis=-1, keepdims=True)
            probs_half = probs.astype(BF16)
            ctx_ref[toks, cols] = mm(probs_half, v, 1, 0).astype(BF16)
            d_probs = mm(g, v, 1, 1)
            delta = jnp.sum(probs * d_probs, axis=-1, keepdims=True)
            d_scores = (probs * (d_probs - delta) * scale_factor).astype(BF16)
            dq_ref[toks, cols] = mm(d_scores, k, 1, 0).astype(BF16)
            dk_ref[poss, cols] = mm(d_scores, q, 0, 0).astype(BF16)
            dv_ref[poss, cols] = mm(probs_half, g, 0, 0).astype(BF16)
    dk = dk_ref[...]
    dv = dv_ref[...]
    dnormed_ref[...] += mm(dk, wk_ref[...], 1, 1) + mm(dv, wv_ref[...], 1, 1)
    shape = own_k_ref.shape
    for grad, own_ref, oth_ref in ((dk, own_k_ref, oth_k_ref), (dv, own_v_ref, oth_v_ref)):
        term = mm(normed_t_ref[...], grad, 1, 0).astype(BF16)
        term = term.reshape(shape[0], 2, shape[1], shape[2])

        @pl.when(core_ref[0] == 0)
        def _():
            own_ref[...] = term[:, 0]
            oth_ref[...] = term[:, 1]

        @pl.when(core_ref[0] != 0)
        def _():
            own_ref[...] = term[:, 1]
            oth_ref[...] = term[:, 0]

    @pl.when(step == pl.num_programs(0) - 1)
    def _():
        for c in range(spans):
            x = wide_rows(c)
            r = lax.rsqrt(jnp.mean(x * x, axis=-1, keepdims=True) + EPSILON)
            dng = dnormed_ref[pl.ds(c * positions, positions), :] * gain
            inner = jnp.sum(dng * x, axis=-1, keepdims=True)
            dx = r * dng - x * (r * r * r * inner * (1.0 / width))
            dfet_ref[:, c] = dx.astype(BF16).reshape(dfet_ref.shape[0], *dfet_ref.shape[2:])


def ring_sum(blocks, axis, position, plus, minus):
    b = [
        lax.dynamic_index_in_dim(blocks, (position + d) % 4, axis, keepdims=False)
        for d in range(4)
    ]
    half = blocks.shape[-1] // 2
    up = lax.ppermute(b[2][..., :half], "nbr", plus)
    down = lax.ppermute(b[2][..., half:], "nbr", minus)
    first = jnp.concatenate([b[1][..., :half] + up, b[1][..., half:]], axis=-1)
    third = jnp.concatenate([b[3][..., :half], b[3][..., half:] + down], axis=-1)
    from_low = lax.ppermute(first, "nbr", plus)
    from_high = lax.ppermute(third, "nbr", minus)
    total = b[0].astype(F32) + from_low.astype(F32) + from_high.astype(F32)
    return total.astype(BF16)


def swap(array):
    return lax.all_to_all(array, "seq", split_axis=0, concat_axis=0, tiled=True)


def body(queries, d_context, database, neighbour_source, neighbour_slot, enc_gain, kv_weight):
    peers = lax.axis_size("seq")
    spans = neighbour_source.shape[0]
    requests = spans * K_NBR
    stored, row_length, width = database.shape
    piece = row_length // peers
    span_length = queries.shape[0] // spans
    kv_width = kv_weight.shape[1] // 2
    me = lax.axis_index("nbr")
    core = me % 2
    x_at = (me // 2) % X_CHIPS
    y_at = me // (2 * X_CHIPS)
    chips = X_CHIPS * Y_CHIPS
    shard_rows = kv_weight.shape[0]

    weight_full = lax.all_gather(kv_weight, "nbr", axis=0, tiled=True)

    wanted = (neighbour_source * stored + neighbour_slot).reshape(1, 1, requests)
    note = jnp.pad(wanted.astype(BF16), ((0, 0), (0, 7), (0, width - requests)))
    note = jnp.broadcast_to(note, (peers, 8, width))
    pieces = database.reshape(stored, peers, piece, width).transpose(1, 0, 2, 3)
    pieces = pieces.reshape(peers, stored * piece, width)
    held = swap(jnp.concatenate([pieces, note], axis=1))
    ids = held[:, stored * piece, :requests].astype(jnp.int32).reshape(peers * requests)
    ids = jnp.clip(ids, 0, peers * stored - 1)

    smem = pl.BlockSpec(memory_space=pltpu.SMEM)
    vmem = pl.BlockSpec(memory_space=pltpu.VMEM)
    picked = pl.pallas_call(
        functools.partial(pick_kernel, peers=peers, stored=stored, requests=requests, piece=piece),
        out_shape=jax.ShapeDtypeStruct((peers, requests * piece, width), BF16),
        in_specs=[smem, vmem],
        out_specs=vmem,
        compiler_params=pltpu.CompilerParams(vmem_limit_bytes=16 << 20),
        cost_estimate=pl.CostEstimate(flops=0, bytes_accessed=4 << 20, transcendentals=0),
        name="pick",
    )(ids, held)
    rows = swap(picked).reshape(peers, spans, K_NBR * piece, width)

    tokens = requests * row_length
    step_cols = HEADS_STEP * HEAD_DIM
    steps = kv_width // step_cols
    half_shape = jax.ShapeDtypeStruct((chips, shard_rows, kv_width), BF16)
    half_spec = pl.BlockSpec((chips, shard_rows, step_cols), lambda i: (0, 0, i))
    token_spec = pl.BlockSpec((queries.shape[0], step_cols), lambda i: (0, i))
    whole = pl.BlockSpec(rows.shape, lambda i: (0, 0, 0, 0))
    context, d_queries, own_k, oth_k, own_v, oth_v, d_rows = pl.pallas_call(
        functools.partial(main_kernel, spans=spans, span_length=span_length),
        grid=(steps,),
        out_shape=[
            jax.ShapeDtypeStruct(queries.shape, BF16),
            jax.ShapeDtypeStruct(queries.shape, BF16),
            half_shape,
            half_shape,
            half_shape,
            half_shape,
            jax.ShapeDtypeStruct(rows.shape, BF16),
        ],
        in_specs=[
            smem,
            whole,
            pl.BlockSpec((1, width), lambda i: (0, 0)),
            pl.BlockSpec((width, step_cols), lambda i: (0, i)),
            pl.BlockSpec((width, step_cols), lambda i: (0, steps + i)),
            token_spec,
            token_spec,
        ],
        out_specs=[token_spec, token_spec, half_spec, half_spec, half_spec, half_spec, whole],
        scratch_shapes=[
            pltpu.VMEM((tokens, width), BF16),
            pltpu.VMEM((width, tokens), BF16),
            pltpu.VMEM((tokens, width), F32),
            pltpu.VMEM((tokens, step_cols), BF16),
            pltpu.VMEM((tokens, step_cols), BF16),
        ],
        compiler_params=pltpu.CompilerParams(vmem_limit_bytes=48 << 20),
        cost_estimate=pl.CostEstimate(
            flops=14_000_000_000, bytes_accessed=24 << 20, transcendentals=1 << 20
        ),
        name="attend",
    )(core.reshape(1), rows, enc_gain.reshape(1, width), weight_full, weight_full, queries, d_context)

    returned = swap(d_rows.reshape(peers, requests * piece, width))

    pair = [(i, i ^ 1) for i in range(2 * chips)]

    def shifted(dx, dy):
        moves = []
        for y in range(Y_CHIPS):
            for x in range(X_CHIPS):
                for k in range(2):
                    to_chip = ((y + dy) % Y_CHIPS) * X_CHIPS + (x + dx) % X_CHIPS
                    moves.append(((y * X_CHIPS + x) * 2 + k, to_chip * 2 + k))
        return moves

    grid4 = (Y_CHIPS, X_CHIPS, shard_rows, kv_width)
    got_k = lax.ppermute(oth_k, "nbr", pair)
    got_v = lax.ppermute(oth_v, "nbr", pair)
    sum_k = (own_k.astype(F32) + got_k.astype(F32)).astype(BF16).reshape(grid4)
    sum_v = (own_v.astype(F32) + got_v.astype(F32)).astype(BF16).reshape(grid4)
    xp, xm, yp, ym = shifted(1, 0), shifted(-1, 0), shifted(0, 1), shifted(0, -1)
    part_k = ring_sum(sum_k, 1, x_at, xp, xm)
    part_v = ring_sum(sum_v, 0, y_at, yp, ym)
    part_k = ring_sum(part_k, 0, y_at, yp, ym)
    part_v = ring_sum(part_v, 0, x_at, xp, xm)
    part = jnp.concatenate([part_k, part_v], axis=1)
    cut = part.shape[1] // peers
    part = swap(part.reshape(shard_rows, peers, cut).transpose(1, 0, 2))
    part = jnp.sum(part.astype(F32), axis=0)
    part = swap(jnp.broadcast_to(part[None], (peers, shard_rows, cut)))
    d_kv_weight = part.transpose(1, 0, 2).reshape(shard_rows, peers * cut)

    summed = pl.pallas_call(
        functools.partial(sum_kernel, peers=peers, requests=requests, piece=piece),
        out_shape=jax.ShapeDtypeStruct((peers, stored * piece, width), BF16),
        in_specs=[smem, vmem],
        out_specs=vmem,
        scratch_shapes=[pltpu.VMEM((peers * stored, piece, width), F32)],
        compiler_params=pltpu.CompilerParams(vmem_limit_bytes=16 << 20),
        cost_estimate=pl.CostEstimate(flops=0, bytes_accessed=4 << 20, transcendentals=0),
        name="add_rows",
    )(ids, returned)
    final = swap(summed).reshape(peers, stored, piece, width)
    d_database = final.transpose(1, 0, 2, 3).reshape(database.shape).astype(F32)
    return context, d_queries, d_kv_weight, d_database


def solution(mesh):
    return jax.shard_map(
        body,
        mesh=mesh,
        in_specs=(
            P(("seq", "nbr"), None),
            P(("seq", "nbr"), None),
            P(("seq", "nbr"), None, None),
            P(("seq", "nbr"), None),
            P(("seq", "nbr"), None),
            P(),
            P("nbr", None),
        ),
        out_specs=(
            P(("seq", "nbr"), None),
            P(("seq", "nbr"), None),
            P("nbr", None),
            P(("seq", "nbr"), None, None),
        ),
        check_vma=False,
    )
```

```python
import functools

import jax
import jax.numpy as jnp
from jax import lax
from jax.experimental import pallas as pl
from jax.experimental.pallas import tpu as pltpu
from jax.sharding import PartitionSpec as P

HEAD_DIM = 128
K_NBR = 2
EPSILON = 1e-06
HEADS_STEP = 4
CHUNKS = 1
X_CHIPS = 4
Y_CHIPS = 4
F32 = jnp.float32
BF16 = jnp.bfloat16


def mm(a, b, ca, cb):
    return lax.dot_general(a, b, (((ca,), (cb,)), ((), ())), preferred_element_type=F32)


def pick_kernel(ids_ref, stored_ref, out_ref, *, peers, stored, requests, piece):
    for peer in range(peers):
        for r in range(requests):
            row = ids_ref[peer * requests + r]
            source = lax.div(row, stored)
            start = pl.multiple_of(lax.rem(row, stored) * piece, piece)
            out_ref[peer, pl.ds(r * piece, piece), :] = stored_ref[source, pl.ds(start, piece), :]


def sum_kernel(ids_ref, grads_ref, out_ref, total_ref, *, peers, requests, piece):
    total_ref[...] = jnp.zeros_like(total_ref)
    for peer in range(peers):
        for r in range(requests):
            row = ids_ref[peer * requests + r]
            total_ref[row] += grads_ref[peer, pl.ds(r * piece, piece), :].astype(F32)
    out_ref[...] = total_ref[...].astype(BF16).reshape(out_ref.shape)


def pair_kernel(at_ref, own_ref, got_ref, stay_ref, next_ref, prev_ref, up_ref, down_ref):
    half = up_ref.shape[0]

    def total(d):
        at = lax.rem(at_ref[0] + d, 4)
        return (own_ref[at].astype(F32) + got_ref[at].astype(F32)).astype(BF16)

    stay_ref[...] = total(0)
    next_ref[...] = total(1)
    prev_ref[...] = total(3)
    far = total(2)
    up_ref[...] = far[:half]
    down_ref[...] = far[half:]


def pair_call(at, own, got):
    ring, chips, rows, cols = own.shape
    width = 512
    whole = pl.BlockSpec((ring, chips, rows, width), lambda i: (0, 0, 0, i))
    block = pl.BlockSpec((chips, rows, width), lambda i: (0, 0, i))
    half = pl.BlockSpec((chips // 2, rows, width), lambda i: (0, 0, i))
    block_shape = jax.ShapeDtypeStruct((chips, rows, cols), BF16)
    half_shape = jax.ShapeDtypeStruct((chips // 2, rows, cols), BF16)
    return pl.pallas_call(
        pair_kernel,
        grid=(cols // width,),
        out_shape=[block_shape] * 3 + [half_shape] * 2,
        in_specs=[pl.BlockSpec(memory_space=pltpu.SMEM), whole, whole],
        out_specs=[block] * 3 + [half] * 2,
        compiler_params=pltpu.CompilerParams(vmem_limit_bytes=58 << 20),
        cost_estimate=pl.CostEstimate(flops=0, bytes_accessed=1 << 10, transcendentals=0),
        name="pair_add",
    )(at, own, got)


def main_kernel(*refs, spans, span_length, chunk):
    core_ref, rows_ref, gain_ref, wk_ref, wv_ref, q_ref, g_ref = refs[:7]
    normed_ref, normed_t_ref, dnormed_ref, dk_ref, dv_ref = refs[-5:]
    ctx_ref, dq_ref, own_ref, oth_ref, final_ref = refs[-10:-5]
    step = pl.program_id(0)
    scale_factor = HEAD_DIM ** (-0.5)
    positions = normed_ref.shape[0] // spans
    width = rows_ref.shape[-1]
    gain = gain_ref[...]

    def wide_rows(c):
        return rows_ref[:, c].astype(F32).reshape(positions, width)

    @pl.when(step == 0)
    def _():
        for c in range(spans):
            x = wide_rows(c)
            r = lax.rsqrt(jnp.mean(x * x, axis=-1, keepdims=True) + EPSILON)
            normed = (x * r * gain).astype(BF16)
            normed_ref[pl.ds(c * positions, positions), :] = normed
            normed_t_ref[:, pl.ds(c * positions, positions)] = normed.T
        if chunk:
            dnormed_ref[...] = refs[7][...]
        else:
            dnormed_ref[...] = jnp.zeros_like(dnormed_ref)

    normed = normed_ref[...]
    keys = mm(normed, wk_ref[...], 1, 0).astype(BF16)
    values = mm(normed, wv_ref[...], 1, 0).astype(BF16)
    blocks = [
        (
            slice(c * span_length, (c + 1) * span_length),
            slice(c * positions, (c + 1) * positions),
            slice(h * HEAD_DIM, (h + 1) * HEAD_DIM),
        )
        for c in range(spans)
        for h in range(HEADS_STEP)
    ]
    scores = jnp.concatenate(
        [mm(q_ref[toks, cols], keys[poss, cols], 1, 1) for toks, poss, cols in blocks], axis=0
    )
    d_probs = jnp.concatenate(
        [mm(g_ref[toks, cols], values[poss, cols], 1, 1) for toks, poss, cols in blocks], axis=0
    )
    scores = scores * scale_factor
    expanded = jnp.exp(scores - jnp.max(scores, axis=-1, keepdims=True))
    probs = expanded * (1.0 / jnp.sum(expanded, axis=-1, keepdims=True))
    delta = jnp.sum(probs * d_probs, axis=-1, keepdims=True)
    probs_half = probs.astype(BF16)
    d_scores = (probs * (d_probs - delta) * scale_factor).astype(BF16)
    for n, (toks, poss, cols) in enumerate(blocks):
        own = slice(n * span_length, (n + 1) * span_length)
        ctx_ref[toks, cols] = mm(probs_half[own], values[poss, cols], 1, 0).astype(BF16)
        dq_ref[toks, cols] = mm(d_scores[own], keys[poss, cols], 1, 0).astype(BF16)
        dk_ref[poss, cols] = mm(d_scores[own], q_ref[toks, cols], 0, 0).astype(BF16)
        dv_ref[poss, cols] = mm(probs_half[own], g_ref[toks, cols], 0, 0).astype(BF16)
    dk = dk_ref[...]
    dv = dv_ref[...]
    dnormed_ref[...] += mm(dk, wk_ref[...], 1, 1) + mm(dv, wv_ref[...], 1, 1)
    rows, cols = own_ref.shape[-2:]
    for kind, grad in enumerate((dk, dv)):
        term = mm(normed_t_ref[...], grad, 1, 0).astype(BF16)
        term = term.reshape(Y_CHIPS, X_CHIPS, rows, cols)

        def put(ref):
            for y in range(Y_CHIPS):
                for x in range(X_CHIPS):
                    at = (x, y) if kind == 0 else (y, x)
                    ref[at] = term[y, x]

        @pl.when(core_ref[0] == kind)
        def _():
            put(own_ref)

        @pl.when(core_ref[0] != kind)
        def _():
            put(oth_ref)

    @pl.when(step == pl.num_programs(0) - 1)
    def _():
        if chunk < CHUNKS - 1:
            final_ref[...] = dnormed_ref[...]
            return
        for c in range(spans):
            x = wide_rows(c)
            r = lax.rsqrt(jnp.mean(x * x, axis=-1, keepdims=True) + EPSILON)
            dng = dnormed_ref[pl.ds(c * positions, positions), :] * gain
            inner = jnp.sum(dng * x, axis=-1, keepdims=True)
            dx = r * dng - x * (r * r * r * inner * (1.0 / width))
            final_ref[:, c] = dx.astype(BF16).reshape(final_ref.shape[0], *final_ref.shape[2:])


def attend_call(core, rows, gain, weight, queries, d_context, chunk, carried):
    peers, spans, run, width = rows.shape
    tokens = peers * spans * run
    span_length = queries.shape[0] // spans
    kv_width = queries.shape[1]
    step_cols = HEADS_STEP * HEAD_DIM
    steps = kv_width // (CHUNKS * step_cols)
    at = chunk * steps
    half = (X_CHIPS, Y_CHIPS, width // (X_CHIPS * Y_CHIPS))
    half_shape = jax.ShapeDtypeStruct((*half, kv_width // CHUNKS), BF16)
    half_spec = pl.BlockSpec((*half, step_cols), lambda i: (0, 0, 0, i))
    token_shape = jax.ShapeDtypeStruct(queries.shape, BF16)
    token_spec = pl.BlockSpec((queries.shape[0], step_cols), lambda i: (0, at + i))
    whole = pl.BlockSpec(rows.shape, lambda i: (0, 0, 0, 0))
    wide_spec = pl.BlockSpec((tokens, width), lambda i: (0, 0))
    last = chunk == CHUNKS - 1
    any_spec = pl.BlockSpec(memory_space=pl.ANY)
    more = [] if chunk == 0 else list(carried)
    return pl.pallas_call(
        functools.partial(main_kernel, spans=spans, span_length=span_length, chunk=chunk),
        grid=(steps,),
        out_shape=[
            token_shape,
            token_shape,
            half_shape,
            half_shape,
            jax.ShapeDtypeStruct(rows.shape, BF16)
            if last
            else jax.ShapeDtypeStruct((tokens, width), F32),
        ],
        in_specs=[
            pl.BlockSpec(memory_space=pltpu.SMEM),
            whole,
            pl.BlockSpec((1, width), lambda i: (0, 0)),
            pl.BlockSpec((width, step_cols), lambda i: (0, at + i)),
            pl.BlockSpec((width, step_cols), lambda i: (0, CHUNKS * steps + at + i)),
            token_spec,
            token_spec,
        ]
        + ([wide_spec, any_spec, any_spec] if more else []),
        out_specs=[token_spec, token_spec, half_spec, half_spec, whole if last else wide_spec],
        scratch_shapes=[
            pltpu.VMEM((tokens, width), BF16),
            pltpu.VMEM((width, tokens), BF16),
            pltpu.VMEM((tokens, width), F32),
            pltpu.VMEM((tokens, step_cols), BF16),
            pltpu.VMEM((tokens, step_cols), BF16),
        ],
        input_output_aliases={8: 0, 9: 1} if more else {},
        compiler_params=pltpu.CompilerParams(vmem_limit_bytes=58 << 20),
        cost_estimate=pl.CostEstimate(
            flops=14_000_000_000 // CHUNKS,
            bytes_accessed=24 << 20,
            transcendentals=(1 << 20) // CHUNKS,
        ),
        name="attend",
    )(core, rows, gain, weight, weight, queries, d_context, *more)


def ring_sum(blocks, position, plus, minus):
    b = [
        lax.dynamic_index_in_dim(blocks, (position + d) % 4, 0, keepdims=False) for d in range(4)
    ]
    half = b[0].shape[0] // 2
    up = lax.ppermute(b[2][:half], "nbr", plus)
    down = lax.ppermute(b[2][half:], "nbr", minus)
    first = lax.dynamic_update_slice(b[1], b[1][:half] + up, (0,) * b[1].ndim)
    third = lax.dynamic_update_slice(b[3], b[3][half:] + down, (half,) + (0,) * (b[3].ndim - 1))
    from_low = lax.ppermute(first, "nbr", plus)
    from_high = lax.ppermute(third, "nbr", minus)
    total = b[0].astype(F32) + from_low.astype(F32) + from_high.astype(F32)
    return total.astype(BF16)


def swap(array):
    return lax.all_to_all(array, "seq", split_axis=0, concat_axis=0, tiled=True)


def body(queries, d_context, database, neighbour_source, neighbour_slot, enc_gain, kv_weight):
    peers = lax.axis_size("seq")
    spans = neighbour_source.shape[0]
    requests = spans * K_NBR
    stored, row_length, width = database.shape
    piece = row_length // peers
    kv_width = kv_weight.shape[1] // 2
    me = lax.axis_index("nbr")
    core = me % 2
    x_at = (me // 2) % X_CHIPS
    y_at = me // (2 * X_CHIPS)
    chips = X_CHIPS * Y_CHIPS
    shard_rows = kv_weight.shape[0]

    weight_full = lax.all_gather(kv_weight, "nbr", axis=0, tiled=True)

    wanted = (neighbour_source * stored + neighbour_slot).reshape(1, 1, requests)
    note = jnp.pad(wanted.astype(BF16), ((0, 0), (0, 7), (0, width - requests)))
    note = jnp.broadcast_to(note, (peers, 8, width))
    pieces = database.reshape(stored, peers, piece, width).transpose(1, 0, 2, 3)
    pieces = pieces.reshape(peers, stored * piece, width)
    held = swap(jnp.concatenate([pieces, note], axis=1))
    ids = held[:, stored * piece, :requests].astype(jnp.int32).reshape(peers * requests)
    ids = jnp.clip(ids, 0, peers * stored - 1)

    smem = pl.BlockSpec(memory_space=pltpu.SMEM)
    vmem = pl.BlockSpec(memory_space=pltpu.VMEM)
    picked = pl.pallas_call(
        functools.partial(pick_kernel, peers=peers, stored=stored, requests=requests, piece=piece),
        out_shape=jax.ShapeDtypeStruct((peers, requests * piece, width), BF16),
        in_specs=[smem, vmem],
        out_specs=vmem,
        compiler_params=pltpu.CompilerParams(vmem_limit_bytes=16 << 20),
        cost_estimate=pl.CostEstimate(flops=0, bytes_accessed=4 << 20, transcendentals=0),
        name="pick",
    )(ids, held)
    rows = swap(picked).reshape(peers, spans, K_NBR * piece, width)

    gain = enc_gain.reshape(1, width)
    core_ref = core.reshape(1)
    carried, owns, oths = None, [], []
    for chunk in range(CHUNKS):
        context, d_queries, own, oth, carry = attend_call(
            core_ref, rows, gain, weight_full, queries, d_context, chunk, carried
        )
        owns.append(own)
        oths.append(oth)
        carried = (carry, context, d_queries)

    returned = swap(carry.reshape(peers, requests * piece, width))

    pair = [(i, i ^ 1) for i in range(2 * chips)]

    def shifted(stage, by):
        moves = []
        for y in range(Y_CHIPS):
            for x in range(X_CHIPS):
                for k in range(2):
                    if (k + stage) % 2 == 0:
                        to_chip = y * X_CHIPS + (x + by) % X_CHIPS
                    else:
                        to_chip = ((y + by) % Y_CHIPS) * X_CHIPS + x
                    moves.append(((y * X_CHIPS + x) * 2 + k, to_chip * 2 + k))
        return moves

    first_at = jnp.where(core == 0, x_at, y_at)
    second_at = jnp.where(core == 0, y_at, x_at)
    plus, minus = shifted(0, 1), shifted(0, -1)
    got = lax.ppermute(oth, "nbr", pair)
    stay, ahead, behind, up, down = pair_call(first_at.reshape(1), own, got)
    half = up.shape[0]
    up = lax.ppermute(up, "nbr", plus)
    down = lax.ppermute(down, "nbr", minus)
    ahead = lax.dynamic_update_slice(ahead, ahead[:half] + up, (0, 0, 0))
    behind = lax.dynamic_update_slice(behind, behind[half:] + down, (half, 0, 0))

    summed = pl.pallas_call(
        functools.partial(sum_kernel, peers=peers, requests=requests, piece=piece),
        out_shape=jax.ShapeDtypeStruct((peers, stored * piece, width), BF16),
        in_specs=[smem, vmem],
        out_specs=vmem,
        scratch_shapes=[pltpu.VMEM((peers * stored, piece, width), F32)],
        compiler_params=pltpu.CompilerParams(vmem_limit_bytes=16 << 20),
        cost_estimate=pl.CostEstimate(flops=0, bytes_accessed=4 << 20, transcendentals=0),
        name="add_rows",
    )(ids, returned)
    low = lax.ppermute(ahead, "nbr", plus)
    high = lax.ppermute(behind, "nbr", minus)
    part = (stay.astype(F32) + low.astype(F32) + high.astype(F32)).astype(BF16)
    part, summed = lax.optimization_barrier((part, summed))
    final = swap(summed)
    part = ring_sum(part, second_at, shifted(1, 1), shifted(1, -1))

    part = part.reshape(2, shard_rows, kv_width)
    keep = lax.dynamic_index_in_dim(part, core, 0, keepdims=False)
    give = lax.dynamic_index_in_dim(part, 1 - core, 0, keepdims=False)
    got = lax.ppermute(give, "nbr", pair)
    keep, got, final = lax.optimization_barrier((keep, got, final))
    final = final.reshape(peers, stored, piece, width)
    d_database = final.transpose(1, 0, 2, 3).reshape(database.shape).astype(F32)

    first = jnp.where(core == 0, keep, got).reshape(peers // 2, -1, kv_width)
    second = jnp.where(core == 0, got, keep).reshape(peers // 2, -1, kv_width)
    terms = swap(jnp.concatenate([first, second], axis=0))
    total = jnp.sum(terms.astype(F32), axis=0, keepdims=True).astype(BF16)
    totals = swap(jnp.broadcast_to(total, terms.shape)).astype(F32)
    totals = totals.reshape(2, shard_rows, kv_width)
    d_kv_weight = jnp.concatenate([totals[0], totals[1]], axis=1)
    return context, d_queries, d_kv_weight, d_database


def solution(mesh):
    return jax.shard_map(
        body,
        mesh=mesh,
        in_specs=(
            P(("seq", "nbr"), None),
            P(("seq", "nbr"), None),
            P(("seq", "nbr"), None, None),
            P(("seq", "nbr"), None),
            P(("seq", "nbr"), None),
            P(),
            P("nbr", None),
        ),
        out_specs=(
            P(("seq", "nbr"), None),
            P(("seq", "nbr"), None),
            P("nbr", None),
            P(("seq", "nbr"), None, None),
        ),
        check_vma=False,
    )
```

```python
import functools

import jax
import jax.numpy as jnp
from jax import lax
from jax.experimental import pallas as pl
from jax.experimental.pallas import tpu as pltpu
from jax.sharding import PartitionSpec as P

HEAD_DIM = 128
K_NBR = 2
EPSILON = 1e-06
HEADS_STEP = 4
CHUNKS = 1
X_CHIPS = 4
Y_CHIPS = 4
F32 = jnp.float32
BF16 = jnp.bfloat16


def mm(a, b, ca, cb):
    return lax.dot_general(a, b, (((ca,), (cb,)), ((), ())), preferred_element_type=F32)


def pick_kernel(ids_ref, stored_ref, out_ref, *, peers, stored, requests, piece):
    for peer in range(peers):
        for r in range(requests):
            row = ids_ref[peer * requests + r]
            source = lax.div(row, stored)
            start = pl.multiple_of(lax.rem(row, stored) * piece, piece)
            out_ref[peer, pl.ds(r * piece, piece), :] = stored_ref[source, pl.ds(start, piece), :]


def sum_kernel(ids_ref, grads_ref, out_ref, total_ref, *, peers, requests, piece):
    total_ref[...] = jnp.zeros_like(total_ref)
    for peer in range(peers):
        for r in range(requests):
            row = ids_ref[peer * requests + r]
            total_ref[row] += grads_ref[peer, pl.ds(r * piece, piece), :].astype(F32)
    out_ref[...] = total_ref[...].astype(BF16).reshape(out_ref.shape)


def pair_kernel(at_ref, own_ref, got_ref, stay_ref, *half_refs):
    def total(d):
        at = lax.rem(at_ref[0] + d, 4)
        return (own_ref[at].astype(F32) + got_ref[at].astype(F32)).astype(BF16)

    stay_ref[...] = total(0)
    for n in range(3):
        block = total(n + 1)
        half = block.shape[0] // 2
        half_refs[2 * n][...] = block[:half]
        half_refs[2 * n + 1][...] = block[half:]


def pair_call(at, own, got):
    ring, chips, rows, cols = own.shape
    width = 512
    whole = pl.BlockSpec((ring, chips, rows, width), lambda i: (0, 0, 0, i))
    block = pl.BlockSpec((chips, rows, width), lambda i: (0, 0, i))
    half = pl.BlockSpec((chips // 2, rows, width), lambda i: (0, 0, i))
    block_shape = jax.ShapeDtypeStruct((chips, rows, cols), BF16)
    half_shape = jax.ShapeDtypeStruct((chips // 2, rows, cols), BF16)
    return pl.pallas_call(
        pair_kernel,
        grid=(cols // width,),
        out_shape=[block_shape] + [half_shape] * 6,
        in_specs=[pl.BlockSpec(memory_space=pltpu.SMEM), whole, whole],
        out_specs=[block] + [half] * 6,
        compiler_params=pltpu.CompilerParams(vmem_limit_bytes=58 << 20),
        cost_estimate=pl.CostEstimate(flops=0, bytes_accessed=1 << 10, transcendentals=0),
        name="pair_add",
    )(at, own, got)


def ring_kernel(at_ref, stay_ref, low_a_ref, low_b_ref, high_a_ref, high_b_ref, *refs):
    out_refs, all_ref = refs[:-1], refs[-1]
    half = low_a_ref.shape[0]
    for n, (low_ref, high_ref) in enumerate(((low_a_ref, high_a_ref), (low_b_ref, high_b_ref))):
        mine = stay_ref[pl.ds(n * half, half)].astype(F32)
        all_ref[pl.ds(n * half, half)] = (
            mine + low_ref[...].astype(F32) + high_ref[...].astype(F32)
        ).astype(BF16)
    for d, out_ref in enumerate(out_refs):
        out_ref[...] = all_ref[lax.rem(at_ref[0] + d, 4)]


def main_kernel(*refs, spans, span_length, chunk):
    core_ref, rows_ref, gain_ref, wk_ref, wv_ref, q_ref, g_ref = refs[:7]
    normed_ref, normed_t_ref, dnormed_ref, dk_ref, dv_ref = refs[-5:]
    ctx_ref, dq_ref, own_ref, oth_ref, final_ref = refs[-10:-5]
    step = pl.program_id(0)
    scale_factor = HEAD_DIM ** (-0.5)
    positions = normed_ref.shape[0] // spans
    width = rows_ref.shape[-1]
    gain = gain_ref[...]

    def wide_rows(c):
        return rows_ref[:, c].astype(F32).reshape(positions, width)

    @pl.when(step == 0)
    def _():
        for c in range(spans):
            x = wide_rows(c)
            r = lax.rsqrt(jnp.mean(x * x, axis=-1, keepdims=True) + EPSILON)
            normed = (x * r * gain).astype(BF16)
            normed_ref[pl.ds(c * positions, positions), :] = normed
            normed_t_ref[:, pl.ds(c * positions, positions)] = normed.T
        if chunk:
            dnormed_ref[...] = refs[7][...]
        else:
            dnormed_ref[...] = jnp.zeros_like(dnormed_ref)

    normed = normed_ref[...]
    keys = mm(normed, wk_ref[...], 1, 0).astype(BF16)
    values = mm(normed, wv_ref[...], 1, 0).astype(BF16)
    blocks = [
        (
            slice(c * span_length, (c + 1) * span_length),
            slice(c * positions, (c + 1) * positions),
            slice(h * HEAD_DIM, (h + 1) * HEAD_DIM),
        )
        for c in range(spans)
        for h in range(HEADS_STEP)
    ]
    scores = jnp.concatenate(
        [mm(q_ref[toks, cols], keys[poss, cols], 1, 1) for toks, poss, cols in blocks], axis=0
    )
    d_probs = jnp.concatenate(
        [mm(g_ref[toks, cols], values[poss, cols], 1, 1) for toks, poss, cols in blocks], axis=0
    )
    scores = scores * scale_factor
    expanded = jnp.exp(scores - jnp.max(scores, axis=-1, keepdims=True))
    probs = expanded * (1.0 / jnp.sum(expanded, axis=-1, keepdims=True))
    delta = jnp.sum(probs * d_probs, axis=-1, keepdims=True)
    probs_half = probs.astype(BF16)
    d_scores = (probs * (d_probs - delta) * scale_factor).astype(BF16)
    for n, (toks, poss, cols) in enumerate(blocks):
        own = slice(n * span_length, (n + 1) * span_length)
        ctx_ref[toks, cols] = mm(probs_half[own], values[poss, cols], 1, 0).astype(BF16)
        dq_ref[toks, cols] = mm(d_scores[own], keys[poss, cols], 1, 0).astype(BF16)
        dk_ref[poss, cols] = mm(d_scores[own], q_ref[toks, cols], 0, 0).astype(BF16)
        dv_ref[poss, cols] = mm(probs_half[own], g_ref[toks, cols], 0, 0).astype(BF16)
    dk = dk_ref[...]
    dv = dv_ref[...]
    dnormed_ref[...] += mm(dk, wk_ref[...], 1, 1) + mm(dv, wv_ref[...], 1, 1)
    rows, cols = own_ref.shape[-2:]
    for kind, grad in enumerate((dk, dv)):
        term = mm(normed_t_ref[...], grad, 1, 0).astype(BF16)
        term = term.reshape(Y_CHIPS, X_CHIPS, rows, cols)

        def put(ref):
            for y in range(Y_CHIPS):
                for x in range(X_CHIPS):
                    at = (x, y) if kind == 0 else (y, x)
                    ref[at] = term[y, x]

        @pl.when(core_ref[0] == kind)
        def _():
            put(own_ref)

        @pl.when(core_ref[0] != kind)
        def _():
            put(oth_ref)

    @pl.when(step == pl.num_programs(0) - 1)
    def _():
        if chunk < CHUNKS - 1:
            final_ref[...] = dnormed_ref[...]
            return
        for c in range(spans):
            x = wide_rows(c)
            r = lax.rsqrt(jnp.mean(x * x, axis=-1, keepdims=True) + EPSILON)
            dng = dnormed_ref[pl.ds(c * positions, positions), :] * gain
            inner = jnp.sum(dng * x, axis=-1, keepdims=True)
            dx = r * dng - x * (r * r * r * inner * (1.0 / width))
            final_ref[:, c] = dx.astype(BF16).reshape(final_ref.shape[0], *final_ref.shape[2:])


def attend_call(core, rows, gain, weight, queries, d_context, chunk, carried):
    peers, spans, run, width = rows.shape
    tokens = peers * spans * run
    span_length = queries.shape[0] // spans
    kv_width = queries.shape[1]
    step_cols = HEADS_STEP * HEAD_DIM
    steps = kv_width // (CHUNKS * step_cols)
    at = chunk * steps
    half = (X_CHIPS, Y_CHIPS, width // (X_CHIPS * Y_CHIPS))
    half_shape = jax.ShapeDtypeStruct((*half, kv_width // CHUNKS), BF16)
    half_spec = pl.BlockSpec((*half, step_cols), lambda i: (0, 0, 0, i))
    token_shape = jax.ShapeDtypeStruct(queries.shape, BF16)
    token_spec = pl.BlockSpec((queries.shape[0], step_cols), lambda i: (0, at + i))
    whole = pl.BlockSpec(rows.shape, lambda i: (0, 0, 0, 0))
    wide_spec = pl.BlockSpec((tokens, width), lambda i: (0, 0))
    last = chunk == CHUNKS - 1
    any_spec = pl.BlockSpec(memory_space=pl.ANY)
    more = [] if chunk == 0 else list(carried)
    return pl.pallas_call(
        functools.partial(main_kernel, spans=spans, span_length=span_length, chunk=chunk),
        grid=(steps,),
        out_shape=[
            token_shape,
            token_shape,
            half_shape,
            half_shape,
            jax.ShapeDtypeStruct(rows.shape, BF16)
            if last
            else jax.ShapeDtypeStruct((tokens, width), F32),
        ],
        in_specs=[
            pl.BlockSpec(memory_space=pltpu.SMEM),
            whole,
            pl.BlockSpec((1, width), lambda i: (0, 0)),
            pl.BlockSpec((width, step_cols), lambda i: (0, at + i)),
            pl.BlockSpec((width, step_cols), lambda i: (0, CHUNKS * steps + at + i)),
            token_spec,
            token_spec,
        ]
        + ([wide_spec, any_spec, any_spec] if more else []),
        out_specs=[token_spec, token_spec, half_spec, half_spec, whole if last else wide_spec],
        scratch_shapes=[
            pltpu.VMEM((tokens, width), BF16),
            pltpu.VMEM((width, tokens), BF16),
            pltpu.VMEM((tokens, width), F32),
            pltpu.VMEM((tokens, step_cols), BF16),
            pltpu.VMEM((tokens, step_cols), BF16),
        ],
        input_output_aliases={8: 0, 9: 1} if more else {},
        compiler_params=pltpu.CompilerParams(vmem_limit_bytes=58 << 20),
        cost_estimate=pl.CostEstimate(
            flops=14_000_000_000 // CHUNKS,
            bytes_accessed=24 << 20,
            transcendentals=(1 << 20) // CHUNKS,
        ),
        name="attend",
    )(core, rows, gain, weight, weight, queries, d_context, *more)


def swap(array):
    return lax.all_to_all(array, "seq", split_axis=0, concat_axis=0, tiled=True)


def body(queries, d_context, database, neighbour_source, neighbour_slot, enc_gain, kv_weight):
    peers = lax.axis_size("seq")
    spans = neighbour_source.shape[0]
    requests = spans * K_NBR
    stored, row_length, width = database.shape
    piece = row_length // peers
    kv_width = kv_weight.shape[1] // 2
    me = lax.axis_index("nbr")
    core = me % 2
    x_at = (me // 2) % X_CHIPS
    y_at = me // (2 * X_CHIPS)
    chips = X_CHIPS * Y_CHIPS
    shard_rows = kv_weight.shape[0]

    weight_full = lax.all_gather(kv_weight, "nbr", axis=0, tiled=True)

    wanted = (neighbour_source * stored + neighbour_slot).reshape(1, 1, requests)
    note = jnp.pad(wanted.astype(BF16), ((0, 0), (0, 7), (0, width - requests)))
    note = jnp.broadcast_to(note, (peers, 8, width))
    pieces = database.reshape(stored, peers, piece, width).transpose(1, 0, 2, 3)
    pieces = pieces.reshape(peers, stored * piece, width)
    held = swap(jnp.concatenate([pieces, note], axis=1))
    ids = held[:, stored * piece, :requests].astype(jnp.int32).reshape(peers * requests)
    ids = jnp.clip(ids, 0, peers * stored - 1)

    smem = pl.BlockSpec(memory_space=pltpu.SMEM)
    vmem = pl.BlockSpec(memory_space=pltpu.VMEM)
    picked = pl.pallas_call(
        functools.partial(pick_kernel, peers=peers, stored=stored, requests=requests, piece=piece),
        out_shape=jax.ShapeDtypeStruct((peers, requests * piece, width), BF16),
        in_specs=[smem, vmem],
        out_specs=vmem,
        compiler_params=pltpu.CompilerParams(vmem_limit_bytes=16 << 20),
        cost_estimate=pl.CostEstimate(flops=0, bytes_accessed=4 << 20, transcendentals=0),
        name="pick",
    )(ids, held)
    rows = swap(picked).reshape(peers, spans, K_NBR * piece, width)

    gain = enc_gain.reshape(1, width)
    core_ref = core.reshape(1)
    carried, owns, oths = None, [], []
    for chunk in range(CHUNKS):
        context, d_queries, own, oth, carry = attend_call(
            core_ref, rows, gain, weight_full, queries, d_context, chunk, carried
        )
        owns.append(own)
        oths.append(oth)
        carried = (carry, context, d_queries)

    returned = swap(carry.reshape(peers, requests * piece, width))

    pair = [(i, i ^ 1) for i in range(2 * chips)]

    def shifted(stage, by):
        moves = []
        for y in range(Y_CHIPS):
            for x in range(X_CHIPS):
                for k in range(2):
                    if (k + stage) % 2 == 0:
                        to_chip = y * X_CHIPS + (x + by) % X_CHIPS
                    else:
                        to_chip = ((y + by) % Y_CHIPS) * X_CHIPS + x
                    moves.append(((y * X_CHIPS + x) * 2 + k, to_chip * 2 + k))
        return moves

    first_at = jnp.where(core == 0, x_at, y_at)
    second_at = jnp.where(core == 0, y_at, x_at)
    plus, minus = shifted(0, 1), shifted(0, -1)
    got = lax.ppermute(oth, "nbr", pair)
    stay, ahead_a, ahead_b, far_a, far_b, behind_a, behind_b = pair_call(
        first_at.reshape(1), own, got
    )
    up = lax.ppermute(far_a, "nbr", plus)
    down = lax.ppermute(far_b, "nbr", minus)
    low_b = lax.ppermute(ahead_b, "nbr", plus)
    high_a = lax.ppermute(behind_a, "nbr", minus)
    ahead_a = ahead_a + up
    behind_b = behind_b + down

    summed = pl.pallas_call(
        functools.partial(sum_kernel, peers=peers, requests=requests, piece=piece),
        out_shape=jax.ShapeDtypeStruct((peers, stored * piece, width), BF16),
        in_specs=[smem, vmem],
        out_specs=vmem,
        scratch_shapes=[pltpu.VMEM((peers * stored, piece, width), F32)],
        compiler_params=pltpu.CompilerParams(vmem_limit_bytes=16 << 20),
        cost_estimate=pl.CostEstimate(flops=0, bytes_accessed=4 << 20, transcendentals=0),
        name="add_rows",
    )(ids, returned)
    ahead_a, behind_b, low_b, high_a, summed = lax.optimization_barrier(
        (ahead_a, behind_b, low_b, high_a, summed)
    )
    final = swap(summed)
    low_a = lax.ppermute(ahead_a, "nbr", plus)
    high_b = lax.ppermute(behind_b, "nbr", minus)
    mine, *others = pl.pallas_call(
        ring_kernel,
        out_shape=[jax.ShapeDtypeStruct(stay.shape[1:], BF16)] * 4,
        in_specs=[smem] + [vmem] * 5,
        out_specs=[vmem] * 4,
        scratch_shapes=[pltpu.VMEM(stay.shape, BF16)],
        compiler_params=pltpu.CompilerParams(vmem_limit_bytes=58 << 20),
        cost_estimate=pl.CostEstimate(flops=0, bytes_accessed=1 << 10, transcendentals=0),
        name="ring_add",
    )(second_at.reshape(1), stay, low_a, low_b, high_a, high_b)
    part = mine.astype(F32)
    for d, other in enumerate(others):
        part = part + lax.ppermute(other, "nbr", shifted(1, d + 1)).astype(F32)
    part = part.astype(BF16)

    part = part.reshape(2, shard_rows, kv_width)
    keep = lax.dynamic_index_in_dim(part, core, 0, keepdims=False)
    give = lax.dynamic_index_in_dim(part, 1 - core, 0, keepdims=False)
    got = lax.ppermute(give, "nbr", pair)
    keep, got, final = lax.optimization_barrier((keep, got, final))
    final = final.reshape(peers, stored, piece, width)
    d_database = final.transpose(1, 0, 2, 3).reshape(database.shape).astype(F32)

    first = jnp.where(core == 0, keep, got).reshape(peers // 2, -1, kv_width)
    second = jnp.where(core == 0, got, keep).reshape(peers // 2, -1, kv_width)
    terms = swap(jnp.concatenate([first, second], axis=0))
    total = jnp.sum(terms.astype(F32), axis=0, keepdims=True).astype(BF16)
    totals = swap(jnp.broadcast_to(total, terms.shape)).astype(F32)
    totals = totals.reshape(2, shard_rows, kv_width)
    d_kv_weight = jnp.concatenate([totals[0], totals[1]], axis=1)
    return context, d_queries, d_kv_weight, d_database


def solution(mesh):
    return jax.shard_map(
        body,
        mesh=mesh,
        in_specs=(
            P(("seq", "nbr"), None),
            P(("seq", "nbr"), None),
            P(("seq", "nbr"), None, None),
            P(("seq", "nbr"), None),
            P(("seq", "nbr"), None),
            P(),
            P("nbr", None),
        ),
        out_specs=(
            P(("seq", "nbr"), None),
            P(("seq", "nbr"), None),
            P("nbr", None),
            P(("seq", "nbr"), None, None),
        ),
        check_vma=False,
    )
```

```python
import functools

import jax
import jax.numpy as jnp
from jax import lax
from jax.experimental import pallas as pl
from jax.experimental.pallas import tpu as pltpu
from jax.sharding import PartitionSpec as P

HEAD_DIM = 128
K_NBR = 2
EPSILON = 1e-06
HEADS_STEP = 4
CHUNKS = 1
X_CHIPS = 4
Y_CHIPS = 4
F32 = jnp.float32
BF16 = jnp.bfloat16


def mm(a, b, ca, cb):
    return lax.dot_general(a, b, (((ca,), (cb,)), ((), ())), preferred_element_type=F32)


def pick_kernel(ids_ref, stored_ref, out_ref, *, peers, stored, requests, piece):
    for peer in range(peers):
        for r in range(requests):
            row = ids_ref[peer * requests + r]
            source = lax.div(row, stored)
            start = pl.multiple_of(lax.rem(row, stored) * piece, piece)
            out_ref[peer, pl.ds(r * piece, piece), :] = stored_ref[source, pl.ds(start, piece), :]


def sum_kernel(ids_ref, grads_ref, out_ref, total_ref, *, peers, requests, piece):
    total_ref[...] = jnp.zeros_like(total_ref)
    for peer in range(peers):
        for r in range(requests):
            row = ids_ref[peer * requests + r]
            total_ref[row] += grads_ref[peer, pl.ds(r * piece, piece), :].astype(F32)
    out_ref[...] = total_ref[...].astype(BF16).reshape(out_ref.shape)


def pair_kernel(at_ref, own_ref, got_ref, stay_ref, *half_refs):
    def total(d):
        at = lax.rem(at_ref[0] + d, 4)
        return (own_ref[at].astype(F32) + got_ref[at].astype(F32)).astype(BF16)

    stay_ref[...] = total(0)
    for n in range(3):
        block = total(n + 1)
        half = block.shape[0] // 2
        half_refs[2 * n][...] = block[:half]
        half_refs[2 * n + 1][...] = block[half:]


def pair_call(at, own, got):
    ring, chips, rows, cols = own.shape
    width = 1024
    whole = pl.BlockSpec((ring, chips, rows, width), lambda i: (0, 0, 0, i))
    block = pl.BlockSpec((chips, rows, width), lambda i: (0, 0, i))
    half = pl.BlockSpec((chips // 2, rows, width), lambda i: (0, 0, i))
    block_shape = jax.ShapeDtypeStruct((chips, rows, cols), BF16)
    half_shape = jax.ShapeDtypeStruct((chips // 2, rows, cols), BF16)
    return pl.pallas_call(
        pair_kernel,
        grid=(cols // width,),
        out_shape=[block_shape] + [half_shape] * 6,
        in_specs=[pl.BlockSpec(memory_space=pltpu.SMEM), whole, whole],
        out_specs=[block] + [half] * 6,
        compiler_params=pltpu.CompilerParams(vmem_limit_bytes=58 << 20),
        cost_estimate=pl.CostEstimate(flops=0, bytes_accessed=1 << 10, transcendentals=0),
        name="pair_add",
    )(at, own, got)


def add_kernel(a_ref, b_ref, c_ref, d_ref, first_ref, second_ref):
    first_ref[...] = (a_ref[...].astype(F32) + b_ref[...].astype(F32)).astype(BF16)
    second_ref[...] = (c_ref[...].astype(F32) + d_ref[...].astype(F32)).astype(BF16)


def ring_kernel(at_ref, stay_ref, low_a_ref, low_b_ref, high_a_ref, high_b_ref, *refs):
    out_refs, all_ref = refs[:-1], refs[-1]
    half = low_a_ref.shape[0]
    for n, (low_ref, high_ref) in enumerate(((low_a_ref, high_a_ref), (low_b_ref, high_b_ref))):
        mine = stay_ref[pl.ds(n * half, half)].astype(F32)
        all_ref[pl.ds(n * half, half)] = (
            mine + low_ref[...].astype(F32) + high_ref[...].astype(F32)
        ).astype(BF16)
    for d, out_ref in enumerate(out_refs):
        out_ref[...] = all_ref[lax.rem(at_ref[0] + d, 4)]


def main_kernel(*refs, spans, span_length, chunk):
    core_ref, rows_ref, gain_ref, wk_ref, wv_ref, q_ref, g_ref = refs[:7]
    normed_ref, normed_t_ref, dnormed_ref, dk_ref, dv_ref = refs[-5:]
    ctx_ref, dq_ref, own_ref, oth_ref, final_ref = refs[-10:-5]
    step = pl.program_id(0)
    scale_factor = HEAD_DIM ** (-0.5)
    positions = normed_ref.shape[0] // spans
    width = rows_ref.shape[-1]
    gain = gain_ref[...]

    def wide_rows(c):
        return rows_ref[:, c].astype(F32).reshape(positions, width)

    @pl.when(step == 0)
    def _():
        for c in range(spans):
            x = wide_rows(c)
            r = lax.rsqrt(jnp.mean(x * x, axis=-1, keepdims=True) + EPSILON)
            normed = (x * r * gain).astype(BF16)
            normed_ref[pl.ds(c * positions, positions), :] = normed
            normed_t_ref[:, pl.ds(c * positions, positions)] = normed.T
        if chunk:
            dnormed_ref[...] = refs[7][...]
        else:
            dnormed_ref[...] = jnp.zeros_like(dnormed_ref)

    normed = normed_ref[...]
    keys = mm(normed, wk_ref[...], 1, 0).astype(BF16)
    values = mm(normed, wv_ref[...], 1, 0).astype(BF16)
    blocks = [
        (
            slice(c * span_length, (c + 1) * span_length),
            slice(c * positions, (c + 1) * positions),
            slice(h * HEAD_DIM, (h + 1) * HEAD_DIM),
        )
        for c in range(spans)
        for h in range(HEADS_STEP)
    ]
    scores = jnp.concatenate(
        [mm(q_ref[toks, cols], keys[poss, cols], 1, 1) for toks, poss, cols in blocks], axis=0
    )
    d_probs = jnp.concatenate(
        [mm(g_ref[toks, cols], values[poss, cols], 1, 1) for toks, poss, cols in blocks], axis=0
    )
    scores = scores * scale_factor
    expanded = jnp.exp(scores - jnp.max(scores, axis=-1, keepdims=True))
    probs = expanded * (1.0 / jnp.sum(expanded, axis=-1, keepdims=True))
    delta = jnp.sum(probs * d_probs, axis=-1, keepdims=True)
    probs_half = probs.astype(BF16)
    d_scores = (probs * (d_probs - delta) * scale_factor).astype(BF16)
    for n, (toks, poss, cols) in enumerate(blocks):
        own = slice(n * span_length, (n + 1) * span_length)
        ctx_ref[toks, cols] = mm(probs_half[own], values[poss, cols], 1, 0).astype(BF16)
        dq_ref[toks, cols] = mm(d_scores[own], keys[poss, cols], 1, 0).astype(BF16)
        dk_ref[poss, cols] = mm(d_scores[own], q_ref[toks, cols], 0, 0).astype(BF16)
        dv_ref[poss, cols] = mm(probs_half[own], g_ref[toks, cols], 0, 0).astype(BF16)
    dk = dk_ref[...]
    dv = dv_ref[...]
    dnormed_ref[...] += mm(dk, wk_ref[...], 1, 1) + mm(dv, wv_ref[...], 1, 1)
    rows, cols = own_ref.shape[-2:]
    for kind, grad in enumerate((dk, dv)):
        term = mm(normed_t_ref[...], grad, 1, 0).astype(BF16)
        term = term.reshape(Y_CHIPS, X_CHIPS, rows, cols)

        def put(ref):
            for y in range(Y_CHIPS):
                for x in range(X_CHIPS):
                    at = (x, y) if kind == 0 else (y, x)
                    ref[at] = term[y, x]

        @pl.when(core_ref[0] == kind)
        def _():
            put(own_ref)

        @pl.when(core_ref[0] != kind)
        def _():
            put(oth_ref)

    @pl.when(step == pl.num_programs(0) - 1)
    def _():
        if chunk < CHUNKS - 1:
            final_ref[...] = dnormed_ref[...]
            return
        for c in range(spans):
            x = wide_rows(c)
            r = lax.rsqrt(jnp.mean(x * x, axis=-1, keepdims=True) + EPSILON)
            dng = dnormed_ref[pl.ds(c * positions, positions), :] * gain
            inner = jnp.sum(dng * x, axis=-1, keepdims=True)
            dx = r * dng - x * (r * r * r * inner * (1.0 / width))
            final_ref[:, c] = dx.astype(BF16).reshape(final_ref.shape[0], *final_ref.shape[2:])


def attend_call(core, rows, gain, weight, queries, d_context, chunk, carried):
    peers, spans, run, width = rows.shape
    tokens = peers * spans * run
    span_length = queries.shape[0] // spans
    kv_width = queries.shape[1]
    step_cols = HEADS_STEP * HEAD_DIM
    steps = kv_width // (CHUNKS * step_cols)
    at = chunk * steps
    half = (X_CHIPS, Y_CHIPS, width // (X_CHIPS * Y_CHIPS))
    half_shape = jax.ShapeDtypeStruct((*half, kv_width // CHUNKS), BF16)
    half_spec = pl.BlockSpec((*half, step_cols), lambda i: (0, 0, 0, i))
    token_shape = jax.ShapeDtypeStruct(queries.shape, BF16)
    token_spec = pl.BlockSpec((queries.shape[0], step_cols), lambda i: (0, at + i))
    whole = pl.BlockSpec(rows.shape, lambda i: (0, 0, 0, 0))
    wide_spec = pl.BlockSpec((tokens, width), lambda i: (0, 0))
    last = chunk == CHUNKS - 1
    any_spec = pl.BlockSpec(memory_space=pl.ANY)
    more = [] if chunk == 0 else list(carried)
    return pl.pallas_call(
        functools.partial(main_kernel, spans=spans, span_length=span_length, chunk=chunk),
        grid=(steps,),
        out_shape=[
            token_shape,
            token_shape,
            half_shape,
            half_shape,
            jax.ShapeDtypeStruct(rows.shape, BF16)
            if last
            else jax.ShapeDtypeStruct((tokens, width), F32),
        ],
        in_specs=[
            pl.BlockSpec(memory_space=pltpu.SMEM),
            whole,
            pl.BlockSpec((1, width), lambda i: (0, 0)),
            pl.BlockSpec((width, step_cols), lambda i: (0, at + i)),
            pl.BlockSpec((width, step_cols), lambda i: (0, CHUNKS * steps + at + i)),
            token_spec,
            token_spec,
        ]
        + ([wide_spec, any_spec, any_spec] if more else []),
        out_specs=[token_spec, token_spec, half_spec, half_spec, whole if last else wide_spec],
        scratch_shapes=[
            pltpu.VMEM((tokens, width), BF16),
            pltpu.VMEM((width, tokens), BF16),
            pltpu.VMEM((tokens, width), F32),
            pltpu.VMEM((tokens, step_cols), BF16),
            pltpu.VMEM((tokens, step_cols), BF16),
        ],
        input_output_aliases={8: 0, 9: 1} if more else {},
        compiler_params=pltpu.CompilerParams(vmem_limit_bytes=50 << 20),
        cost_estimate=pl.CostEstimate(
            flops=14_000_000_000 // CHUNKS,
            bytes_accessed=24 << 20,
            transcendentals=(1 << 20) // CHUNKS,
        ),
        name="attend",
    )(core, rows, gain, weight, weight, queries, d_context, *more)


def swap(array):
    return lax.all_to_all(array, "seq", split_axis=0, concat_axis=0, tiled=True)


def body(queries, d_context, database, neighbour_source, neighbour_slot, enc_gain, kv_weight):
    peers = lax.axis_size("seq")
    spans = neighbour_source.shape[0]
    requests = spans * K_NBR
    stored, row_length, width = database.shape
    piece = row_length // peers
    kv_width = kv_weight.shape[1] // 2
    me = lax.axis_index("nbr")
    core = me % 2
    x_at = (me // 2) % X_CHIPS
    y_at = me // (2 * X_CHIPS)
    chips = X_CHIPS * Y_CHIPS
    shard_rows = kv_weight.shape[0]

    weight_full = lax.all_gather(kv_weight, "nbr", axis=0, tiled=True)

    wanted = (neighbour_source * stored + neighbour_slot).reshape(1, 1, requests)
    note = jnp.pad(wanted.astype(BF16), ((0, 0), (0, 7), (0, width - requests)))
    note = jnp.broadcast_to(note, (peers, 8, width))
    pieces = database.reshape(stored, peers, piece, width).transpose(1, 0, 2, 3)
    pieces = pieces.reshape(peers, stored * piece, width)
    held = swap(jnp.concatenate([pieces, note], axis=1))
    ids = held[:, stored * piece, :requests].astype(jnp.int32).reshape(peers * requests)
    ids = jnp.clip(ids, 0, peers * stored - 1)

    smem = pl.BlockSpec(memory_space=pltpu.SMEM)
    vmem = pl.BlockSpec(memory_space=pltpu.VMEM)
    picked = pl.pallas_call(
        functools.partial(pick_kernel, peers=peers, stored=stored, requests=requests, piece=piece),
        out_shape=jax.ShapeDtypeStruct((peers, requests * piece, width), BF16),
        in_specs=[smem, vmem],
        out_specs=vmem,
        compiler_params=pltpu.CompilerParams(vmem_limit_bytes=16 << 20),
        cost_estimate=pl.CostEstimate(flops=0, bytes_accessed=4 << 20, transcendentals=0),
        name="pick",
    )(ids, held)
    rows = swap(picked).reshape(peers, spans, K_NBR * piece, width)

    gain = enc_gain.reshape(1, width)
    core_ref = core.reshape(1)
    carried, owns, oths = None, [], []
    for chunk in range(CHUNKS):
        context, d_queries, own, oth, carry = attend_call(
            core_ref, rows, gain, weight_full, queries, d_context, chunk, carried
        )
        owns.append(own)
        oths.append(oth)
        carried = (carry, context, d_queries)

    returned = swap(carry.reshape(peers, requests * piece, width))

    pair = [(i, i ^ 1) for i in range(2 * chips)]

    def shifted(stage, by):
        moves = []
        for y in range(Y_CHIPS):
            for x in range(X_CHIPS):
                for k in range(2):
                    if (k + stage) % 2 == 0:
                        to_chip = y * X_CHIPS + (x + by) % X_CHIPS
                    else:
                        to_chip = ((y + by) % Y_CHIPS) * X_CHIPS + x
                    moves.append(((y * X_CHIPS + x) * 2 + k, to_chip * 2 + k))
        return moves

    first_at = jnp.where(core == 0, x_at, y_at)
    second_at = jnp.where(core == 0, y_at, x_at)
    plus, minus = shifted(0, 1), shifted(0, -1)
    got = lax.ppermute(oth, "nbr", pair)
    stay, ahead_a, ahead_b, far_a, far_b, behind_a, behind_b = pair_call(
        first_at.reshape(1), own, got
    )
    up = lax.ppermute(far_a, "nbr", plus)
    down = lax.ppermute(far_b, "nbr", minus)
    low_b = lax.ppermute(ahead_b, "nbr", plus)
    high_a = lax.ppermute(behind_a, "nbr", minus)
    ahead_a, behind_b = pl.pallas_call(
        add_kernel,
        out_shape=[jax.ShapeDtypeStruct(up.shape, BF16)] * 2,
        in_specs=[vmem] * 4,
        out_specs=[vmem] * 2,
        compiler_params=pltpu.CompilerParams(vmem_limit_bytes=58 << 20),
        cost_estimate=pl.CostEstimate(flops=0, bytes_accessed=1 << 10, transcendentals=0),
        name="add_two",
    )(ahead_a, up, behind_b, down)

    summed = pl.pallas_call(
        functools.partial(sum_kernel, peers=peers, requests=requests, piece=piece),
        out_shape=jax.ShapeDtypeStruct((peers, stored * piece, width), BF16),
        in_specs=[smem, vmem],
        out_specs=vmem,
        scratch_shapes=[pltpu.VMEM((peers * stored, piece, width), F32)],
        compiler_params=pltpu.CompilerParams(vmem_limit_bytes=16 << 20),
        cost_estimate=pl.CostEstimate(flops=0, bytes_accessed=4 << 20, transcendentals=0),
        name="add_rows",
    )(ids, returned)
    low_a = lax.ppermute(ahead_a, "nbr", plus)
    high_b = lax.ppermute(behind_b, "nbr", minus)
    low_a, low_b, high_a, high_b, summed = lax.optimization_barrier(
        (low_a, low_b, high_a, high_b, summed)
    )
    final = swap(summed)
    mine, *others = pl.pallas_call(
        ring_kernel,
        out_shape=[jax.ShapeDtypeStruct(stay.shape[1:], BF16)] * 4,
        in_specs=[smem] + [vmem] * 5,
        out_specs=[vmem] * 4,
        scratch_shapes=[pltpu.VMEM(stay.shape, BF16)],
        compiler_params=pltpu.CompilerParams(vmem_limit_bytes=58 << 20),
        cost_estimate=pl.CostEstimate(flops=0, bytes_accessed=1 << 10, transcendentals=0),
        name="ring_add",
    )(second_at.reshape(1), stay, low_a, low_b, high_a, high_b)
    part = mine.astype(F32)
    for d, other in enumerate(others):
        part = part + lax.ppermute(other, "nbr", shifted(1, d + 1)).astype(F32)
    part = part.astype(BF16)

    part = part.reshape(2, shard_rows, kv_width)
    keep = lax.dynamic_index_in_dim(part, core, 0, keepdims=False)
    give = lax.dynamic_index_in_dim(part, 1 - core, 0, keepdims=False)
    got = lax.ppermute(give, "nbr", pair)
    keep, got, final = lax.optimization_barrier((keep, got, final))
    final = final.reshape(peers, stored, piece, width)
    d_database = final.transpose(1, 0, 2, 3).reshape(database.shape).astype(F32)

    first = jnp.where(core == 0, keep, got).reshape(peers // 2, -1, kv_width)
    second = jnp.where(core == 0, got, keep).reshape(peers // 2, -1, kv_width)
    terms = swap(jnp.concatenate([first, second], axis=0))
    total = jnp.sum(terms.astype(F32), axis=0, keepdims=True).astype(BF16)
    totals = swap(jnp.broadcast_to(total, terms.shape)).astype(F32)
    totals = totals.reshape(2, shard_rows, kv_width)
    d_kv_weight = jnp.concatenate([totals[0], totals[1]], axis=1)
    return context, d_queries, d_kv_weight, d_database


def solution(mesh):
    return jax.shard_map(
        body,
        mesh=mesh,
        in_specs=(
            P(("seq", "nbr"), None),
            P(("seq", "nbr"), None),
            P(("seq", "nbr"), None, None),
            P(("seq", "nbr"), None),
            P(("seq", "nbr"), None),
            P(),
            P("nbr", None),
        ),
        out_specs=(
            P(("seq", "nbr"), None),
            P(("seq", "nbr"), None),
            P("nbr", None),
            P(("seq", "nbr"), None, None),
        ),
        check_vma=False,
    )
```

```python
import functools

import jax
import jax.numpy as jnp
from jax import lax
from jax.experimental import pallas as pl
from jax.experimental.pallas import tpu as pltpu
from jax.sharding import PartitionSpec as P

HEAD_DIM = 128
K_NBR = 2
EPSILON = 1e-06
HEADS_STEP = 4
CHUNKS = 1
X_CHIPS = 4
Y_CHIPS = 4
F32 = jnp.float32
BF16 = jnp.bfloat16


def mm(a, b, ca, cb):
    return lax.dot_general(a, b, (((ca,), (cb,)), ((), ())), preferred_element_type=F32)


def pick_kernel(ids_ref, stored_ref, out_ref, *, peers, stored, requests, piece):
    for peer in range(peers):
        for r in range(requests):
            row = ids_ref[peer * requests + r]
            source = lax.div(row, stored)
            start = pl.multiple_of(lax.rem(row, stored) * piece, piece)
            out_ref[peer, pl.ds(r * piece, piece), :] = stored_ref[source, pl.ds(start, piece), :]


def sum_kernel(ids_ref, grads_ref, out_ref, total_ref, *, peers, requests, piece):
    total_ref[...] = jnp.zeros_like(total_ref)
    for peer in range(peers):
        for r in range(requests):
            row = ids_ref[peer * requests + r]
            total_ref[row] += grads_ref[peer, pl.ds(r * piece, piece), :].astype(F32)
    out_ref[...] = total_ref[...].astype(BF16).reshape(out_ref.shape)


def pair_kernel(at_ref, own_ref, got_ref, stay_ref, *half_refs):
    def total(d):
        at = lax.rem(at_ref[0] + d, 4)
        return (own_ref[at].astype(F32) + got_ref[at].astype(F32)).astype(BF16)

    stay_ref[...] = total(0)
    for n in range(3):
        block = total(n + 1)
        half = block.shape[0] // 2
        half_refs[2 * n][...] = block[:half]
        half_refs[2 * n + 1][...] = block[half:]


def pair_call(at, own, got):
    ring, chips, rows, cols = own.shape
    width = 1024
    whole = pl.BlockSpec((ring, chips, rows, width), lambda i: (0, 0, 0, i))
    block = pl.BlockSpec((chips, rows, width), lambda i: (0, 0, i))
    half = pl.BlockSpec((chips // 2, rows, width), lambda i: (0, 0, i))
    block_shape = jax.ShapeDtypeStruct((chips, rows, cols), BF16)
    half_shape = jax.ShapeDtypeStruct((chips // 2, rows, cols), BF16)
    return pl.pallas_call(
        pair_kernel,
        grid=(cols // width,),
        out_shape=[block_shape] + [half_shape] * 6,
        in_specs=[pl.BlockSpec(memory_space=pltpu.SMEM), whole, whole],
        out_specs=[block] + [half] * 6,
        compiler_params=pltpu.CompilerParams(vmem_limit_bytes=58 << 20),
        cost_estimate=pl.CostEstimate(flops=0, bytes_accessed=1 << 10, transcendentals=0),
        name="pair_add",
    )(at, own, got)


def add_kernel(a_ref, b_ref, c_ref, d_ref, first_ref, second_ref):
    first_ref[...] = (a_ref[...].astype(F32) + b_ref[...].astype(F32)).astype(BF16)
    second_ref[...] = (c_ref[...].astype(F32) + d_ref[...].astype(F32)).astype(BF16)


def ring_kernel(at_ref, stay_ref, low_a_ref, low_b_ref, high_a_ref, high_b_ref, *refs):
    out_refs, all_ref = refs[:-1], refs[-1]
    half = low_a_ref.shape[0]
    for n, (low_ref, high_ref) in enumerate(((low_a_ref, high_a_ref), (low_b_ref, high_b_ref))):
        mine = stay_ref[pl.ds(n * half, half)].astype(F32)
        all_ref[pl.ds(n * half, half)] = (
            mine + low_ref[...].astype(F32) + high_ref[...].astype(F32)
        ).astype(BF16)
    for d, out_ref in enumerate(out_refs):
        out_ref[...] = all_ref[lax.rem(at_ref[0] + d, 4)]


def main_kernel(*refs, spans, span_length, chunk):
    core_ref, rows_ref, gain_ref, wk_ref, wv_ref, q_ref, g_ref = refs[:7]
    normed_ref, normed_t_ref, dnormed_ref, dk_ref, dv_ref = refs[-5:]
    ctx_ref, dq_ref, own_ref, oth_ref, final_ref = refs[-10:-5]
    step = pl.program_id(0)
    scale_factor = HEAD_DIM ** (-0.5)
    positions = normed_ref.shape[0] // spans
    width = rows_ref.shape[-1]
    gain = gain_ref[...]

    def wide_rows(c):
        return rows_ref[:, c].astype(F32).reshape(positions, width)

    @pl.when(step == 0)
    def _():
        for c in range(spans):
            x = wide_rows(c)
            r = lax.rsqrt(jnp.mean(x * x, axis=-1, keepdims=True) + EPSILON)
            normed = (x * r * gain).astype(BF16)
            normed_ref[pl.ds(c * positions, positions), :] = normed
            normed_t_ref[:, pl.ds(c * positions, positions)] = normed.T
        if chunk:
            dnormed_ref[...] = refs[7][...]
        else:
            dnormed_ref[...] = jnp.zeros_like(dnormed_ref)

    normed = normed_ref[...]
    keys = mm(normed, wk_ref[...], 1, 0).astype(BF16)
    values = mm(normed, wv_ref[...], 1, 0).astype(BF16)
    blocks = [
        (
            slice(c * span_length, (c + 1) * span_length),
            slice(c * positions, (c + 1) * positions),
            slice(h * HEAD_DIM, (h + 1) * HEAD_DIM),
        )
        for c in range(spans)
        for h in range(HEADS_STEP)
    ]
    scores = jnp.concatenate(
        [mm(q_ref[toks, cols], keys[poss, cols], 1, 1) for toks, poss, cols in blocks], axis=0
    )
    d_probs = jnp.concatenate(
        [mm(g_ref[toks, cols], values[poss, cols], 1, 1) for toks, poss, cols in blocks], axis=0
    )
    scores = scores * scale_factor
    expanded = jnp.exp(scores - jnp.max(scores, axis=-1, keepdims=True))
    probs = expanded * (1.0 / jnp.sum(expanded, axis=-1, keepdims=True))
    delta = jnp.sum(probs * d_probs, axis=-1, keepdims=True)
    probs_half = probs.astype(BF16)
    d_scores = (probs * (d_probs - delta) * scale_factor).astype(BF16)
    for n, (toks, poss, cols) in enumerate(blocks):
        own = slice(n * span_length, (n + 1) * span_length)
        ctx_ref[toks, cols] = mm(probs_half[own], values[poss, cols], 1, 0).astype(BF16)
        dq_ref[toks, cols] = mm(d_scores[own], keys[poss, cols], 1, 0).astype(BF16)
        dk_ref[poss, cols] = mm(d_scores[own], q_ref[toks, cols], 0, 0).astype(BF16)
        dv_ref[poss, cols] = mm(probs_half[own], g_ref[toks, cols], 0, 0).astype(BF16)
    dk = dk_ref[...]
    dv = dv_ref[...]
    dnormed_ref[...] += mm(dk, wk_ref[...], 1, 1) + mm(dv, wv_ref[...], 1, 1)
    rows, cols = own_ref.shape[-2:]
    for kind, grad in enumerate((dk, dv)):
        term = mm(normed_t_ref[...], grad, 1, 0).astype(BF16)
        term = term.reshape(Y_CHIPS, X_CHIPS, rows, cols)

        def put(ref):
            for y in range(Y_CHIPS):
                for x in range(X_CHIPS):
                    at = (x, y) if kind == 0 else (y, x)
                    ref[at] = term[y, x]

        @pl.when(core_ref[0] == kind)
        def _():
            put(own_ref)

        @pl.when(core_ref[0] != kind)
        def _():
            put(oth_ref)

    @pl.when(step == pl.num_programs(0) - 1)
    def _():
        if chunk < CHUNKS - 1:
            final_ref[...] = dnormed_ref[...]
            return
        for c in range(spans):
            x = wide_rows(c)
            r = lax.rsqrt(jnp.mean(x * x, axis=-1, keepdims=True) + EPSILON)
            dng = dnormed_ref[pl.ds(c * positions, positions), :] * gain
            inner = jnp.sum(dng * x, axis=-1, keepdims=True)
            dx = r * dng - x * (r * r * r * inner * (1.0 / width))
            final_ref[:, c] = dx.astype(BF16).reshape(final_ref.shape[0], *final_ref.shape[2:])


def attend_call(core, rows, gain, weight, queries, d_context, chunk, carried):
    peers, spans, run, width = rows.shape
    tokens = peers * spans * run
    span_length = queries.shape[0] // spans
    kv_width = queries.shape[1]
    step_cols = HEADS_STEP * HEAD_DIM
    steps = kv_width // (CHUNKS * step_cols)
    at = chunk * steps
    half = (X_CHIPS, Y_CHIPS, width // (X_CHIPS * Y_CHIPS))
    half_shape = jax.ShapeDtypeStruct((*half, kv_width // CHUNKS), BF16)
    half_spec = pl.BlockSpec((*half, step_cols), lambda i: (0, 0, 0, i))
    token_shape = jax.ShapeDtypeStruct(queries.shape, BF16)
    token_spec = pl.BlockSpec((queries.shape[0], step_cols), lambda i: (0, at + i))
    whole = pl.BlockSpec(rows.shape, lambda i: (0, 0, 0, 0))
    wide_spec = pl.BlockSpec((tokens, width), lambda i: (0, 0))
    last = chunk == CHUNKS - 1
    any_spec = pl.BlockSpec(memory_space=pl.ANY)
    more = [] if chunk == 0 else list(carried)
    return pl.pallas_call(
        functools.partial(main_kernel, spans=spans, span_length=span_length, chunk=chunk),
        grid=(steps,),
        out_shape=[
            token_shape,
            token_shape,
            half_shape,
            half_shape,
            jax.ShapeDtypeStruct(rows.shape, BF16)
            if last
            else jax.ShapeDtypeStruct((tokens, width), F32),
        ],
        in_specs=[
            pl.BlockSpec(memory_space=pltpu.SMEM),
            whole,
            pl.BlockSpec((1, width), lambda i: (0, 0)),
            pl.BlockSpec((width, step_cols), lambda i: (0, at + i)),
            pl.BlockSpec((width, step_cols), lambda i: (0, CHUNKS * steps + at + i)),
            token_spec,
            token_spec,
        ]
        + ([wide_spec, any_spec, any_spec] if more else []),
        out_specs=[token_spec, token_spec, half_spec, half_spec, whole if last else wide_spec],
        scratch_shapes=[
            pltpu.VMEM((tokens, width), BF16),
            pltpu.VMEM((width, tokens), BF16),
            pltpu.VMEM((tokens, width), F32),
            pltpu.VMEM((tokens, step_cols), BF16),
            pltpu.VMEM((tokens, step_cols), BF16),
        ],
        input_output_aliases={8: 0, 9: 1} if more else {},
        compiler_params=pltpu.CompilerParams(vmem_limit_bytes=50 << 20),
        cost_estimate=pl.CostEstimate(
            flops=14_000_000_000 // CHUNKS,
            bytes_accessed=24 << 20,
            transcendentals=(1 << 20) // CHUNKS,
        ),
        name="attend",
    )(core, rows, gain, weight, weight, queries, d_context, *more)


def swap(array):
    return lax.all_to_all(array, "seq", split_axis=0, concat_axis=0, tiled=True)


def body(queries, d_context, database, neighbour_source, neighbour_slot, enc_gain, kv_weight):
    peers = lax.axis_size("seq")
    spans = neighbour_source.shape[0]
    requests = spans * K_NBR
    stored, row_length, width = database.shape
    piece = row_length // peers
    kv_width = kv_weight.shape[1] // 2
    me = lax.axis_index("nbr")
    core = me % 2
    x_at = (me // 2) % X_CHIPS
    y_at = me // (2 * X_CHIPS)
    chips = X_CHIPS * Y_CHIPS
    shard_rows = kv_weight.shape[0]

    weight_full = lax.all_gather(kv_weight, "nbr", axis=0, tiled=True)

    wanted = (neighbour_source * stored + neighbour_slot).reshape(1, 1, requests)
    note = jnp.pad(wanted.astype(BF16), ((0, 0), (0, 7), (0, width - requests)))
    note = jnp.broadcast_to(note, (peers, 8, width))
    pieces = database.reshape(stored, peers, piece, width).transpose(1, 0, 2, 3)
    pieces = pieces.reshape(peers, stored * piece, width)
    held = swap(jnp.concatenate([pieces, note], axis=1))
    ids = held[:, stored * piece, :requests].astype(jnp.int32).reshape(peers * requests)
    ids = jnp.clip(ids, 0, peers * stored - 1)

    smem = pl.BlockSpec(memory_space=pltpu.SMEM)
    vmem = pl.BlockSpec(memory_space=pltpu.VMEM)
    picked = pl.pallas_call(
        functools.partial(pick_kernel, peers=peers, stored=stored, requests=requests, piece=piece),
        out_shape=jax.ShapeDtypeStruct((peers, requests * piece, width), BF16),
        in_specs=[smem, vmem],
        out_specs=vmem,
        compiler_params=pltpu.CompilerParams(vmem_limit_bytes=16 << 20),
        cost_estimate=pl.CostEstimate(flops=0, bytes_accessed=4 << 20, transcendentals=0),
        name="pick",
    )(ids, held)
    rows = swap(picked).reshape(peers, spans, K_NBR * piece, width)

    gain = enc_gain.reshape(1, width)
    core_ref = core.reshape(1)
    carried, owns, oths = None, [], []
    for chunk in range(CHUNKS):
        context, d_queries, own, oth, carry = attend_call(
            core_ref, rows, gain, weight_full, queries, d_context, chunk, carried
        )
        owns.append(own)
        oths.append(oth)
        carried = (carry, context, d_queries)

    returned = swap(carry.reshape(peers, requests * piece, width))

    pair = [(i, i ^ 1) for i in range(2 * chips)]

    def shifted(stage, by):
        moves = []
        for y in range(Y_CHIPS):
            for x in range(X_CHIPS):
                for k in range(2):
                    if (k + stage) % 2 == 0:
                        to_chip = y * X_CHIPS + (x + by) % X_CHIPS
                    else:
                        to_chip = ((y + by) % Y_CHIPS) * X_CHIPS + x
                    moves.append(((y * X_CHIPS + x) * 2 + k, to_chip * 2 + k))
        return moves

    first_at = jnp.where(core == 0, x_at, y_at)
    second_at = jnp.where(core == 0, y_at, x_at)
    plus, minus = shifted(0, 1), shifted(0, -1)
    got = lax.ppermute(oth, "nbr", pair)
    stay, ahead_a, ahead_b, far_a, far_b, behind_a, behind_b = pair_call(
        first_at.reshape(1), own, got
    )
    up = lax.ppermute(far_a, "nbr", plus)
    down = lax.ppermute(far_b, "nbr", minus)
    low_b = lax.ppermute(ahead_b, "nbr", plus)
    high_a = lax.ppermute(behind_a, "nbr", minus)
    add_spec = pl.BlockSpec((1, *up.shape[1:]), lambda i: (i, 0, 0))
    ahead_a, behind_b = pl.pallas_call(
        add_kernel,
        grid=(2,),
        out_shape=[jax.ShapeDtypeStruct(up.shape, BF16)] * 2,
        in_specs=[add_spec] * 4,
        out_specs=[add_spec] * 2,
        compiler_params=pltpu.CompilerParams(vmem_limit_bytes=58 << 20),
        cost_estimate=pl.CostEstimate(flops=0, bytes_accessed=1 << 10, transcendentals=0),
        name="add_two",
    )(ahead_a, up, behind_b, down)

    summed = pl.pallas_call(
        functools.partial(sum_kernel, peers=peers, requests=requests, piece=piece),
        out_shape=jax.ShapeDtypeStruct((peers, stored * piece, width), BF16),
        in_specs=[smem, vmem],
        out_specs=vmem,
        scratch_shapes=[pltpu.VMEM((peers * stored, piece, width), F32)],
        compiler_params=pltpu.CompilerParams(vmem_limit_bytes=16 << 20),
        cost_estimate=pl.CostEstimate(flops=0, bytes_accessed=4 << 20, transcendentals=0),
        name="add_rows",
    )(ids, returned)
    low_a = lax.ppermute(ahead_a, "nbr", plus)
    high_b = lax.ppermute(behind_b, "nbr", minus)
    low_a, low_b, high_a, high_b, summed = lax.optimization_barrier(
        (low_a, low_b, high_a, high_b, summed)
    )
    final = swap(summed)
    mine, *others = pl.pallas_call(
        ring_kernel,
        out_shape=[jax.ShapeDtypeStruct(stay.shape[1:], BF16)] * 4,
        in_specs=[smem] + [vmem] * 5,
        out_specs=[vmem] * 4,
        scratch_shapes=[pltpu.VMEM(stay.shape, BF16)],
        compiler_params=pltpu.CompilerParams(vmem_limit_bytes=58 << 20),
        cost_estimate=pl.CostEstimate(flops=0, bytes_accessed=1 << 10, transcendentals=0),
        name="ring_add",
    )(second_at.reshape(1), stay, low_a, low_b, high_a, high_b)
    part = mine.astype(F32)
    for d, other in enumerate(others):
        part = part + lax.ppermute(other, "nbr", shifted(1, d + 1)).astype(F32)
    part = part.astype(BF16)

    part = part.reshape(2, shard_rows, kv_width)
    keep = lax.dynamic_index_in_dim(part, core, 0, keepdims=False)
    give = lax.dynamic_index_in_dim(part, 1 - core, 0, keepdims=False)
    got = lax.ppermute(give, "nbr", pair)
    keep, got, final = lax.optimization_barrier((keep, got, final))
    final = final.reshape(peers, stored, piece, width)
    d_database = final.transpose(1, 0, 2, 3).reshape(database.shape).astype(F32)

    first = jnp.where(core == 0, keep, got).reshape(peers // 2, -1, kv_width)
    second = jnp.where(core == 0, got, keep).reshape(peers // 2, -1, kv_width)
    terms = swap(jnp.concatenate([first, second], axis=0))
    total = jnp.sum(terms.astype(F32), axis=0, keepdims=True).astype(BF16)
    totals = swap(jnp.broadcast_to(total, terms.shape)).astype(F32)
    totals = totals.reshape(2, shard_rows, kv_width)
    d_kv_weight = jnp.concatenate([totals[0], totals[1]], axis=1)
    return context, d_queries, d_kv_weight, d_database


def solution(mesh):
    return jax.shard_map(
        body,
        mesh=mesh,
        in_specs=(
            P(("seq", "nbr"), None),
            P(("seq", "nbr"), None),
            P(("seq", "nbr"), None, None),
            P(("seq", "nbr"), None),
            P(("seq", "nbr"), None),
            P(),
            P("nbr", None),
        ),
        out_specs=(
            P(("seq", "nbr"), None),
            P(("seq", "nbr"), None),
            P("nbr", None),
            P(("seq", "nbr"), None, None),
        ),
        check_vma=False,
    )
```
